256 devices in a mesh: section: 16 (over z, core), fsdp: 16 (over y, x).
Axes of the slice: x: 4, y: 4, z: 8, core: 2. Of those that a mesh axis runs over, the one named last changes fastest.
Arguments:
- grad: bfloat16 [32, 512, 8192], P('section', 'fsdp'), parts along dimension 0
- left_stat: float32 [512, 512, 512], P(('section', 'fsdp')), parts along dimension 0
- right_stat: float32 [512, 512, 512], P(('section', 'fsdp')), parts along dimension 0
- left_root: bfloat16 [512, 512, 512], P(('section', 'fsdp')), parts along dimension 0
- right_root: bfloat16 [512, 512, 512], P(('section', 'fsdp')), parts along dimension 0
- table: int32 [512], P('section'), parts along dimension 0, may hold values from 0 to 31, each once
Outputs:
- update: bfloat16 [32, 512, 8192], P('section', 'fsdp'), parts along dimension 0
- left_new: float32 [512, 512, 512], P(('section', 'fsdp')), parts along dimension 0
- right_new: float32 [512, 512, 512], P(('section', 'fsdp')), parts along dimension 0
The draws below stay inside these ranges and needn't reach their ends.
There are 16 independent parts, one for each index of `section`. The reference program is written for one: setup_inputs(seed, part) draws one part's arguments, and reference() takes and returns one part's arrays. A program takes and returns all parts, laid end to end along the dimension named above; each array names one. Nothing has to cross between parts.
Inputs may be any that keep to these rules, and one draw needn't show every extreme that they name: `table`: each block number stands in exactly one slot; slot s is kept by fsdp device s // 2.
All inputs are finite; a program needn't handle non-finite values.
Results may differ from the reference program's by a relative error of at most 0.0058.
Values may be sent and summed in bfloat16 or wider, within the bound.
No kernel may reach another device: no remote copies, remote signals or barrier semaphores. Data moves between devices by JAX's collectives and lax.ppermute only.
A program may use at most 64 MiB of HBM per device.

```python
import jax
import jax.numpy as jnp
from jax import lax

D = 8192
BS = 512
NBR = 2
NBLK = 32


def draw_grad(key, part):
    key = jax.random.fold_in(key, 11)
    key_base, key_row, key_col = jax.random.split(key, 3)
    ramp = jnp.arange(BS, dtype=jnp.float32) / BS
    row_scale = 10.0 ** (ramp + 0.15 * jax.random.uniform(key_row, (BS,), jnp.float32))
    col_scale = 10.0 ** jax.random.uniform(key_col, (D,), jnp.float32)
    base = jax.random.normal(key_base, (NBR, BS, D), jnp.float32)
    return (0.1 * base * row_scale[None, :, None] * col_scale[None, None, :]).astype(jnp.bfloat16)


def statistic(noise, key):
    noise = noise * (0.5 / jnp.sqrt(jnp.float32(BS)))
    diag = jax.random.uniform(key, (NBLK, BS), jnp.float32, 1.0, 4.0)
    return noise + jnp.swapaxes(noise, 1, 2) + diag[:, :, None] * jnp.eye(BS, dtype=jnp.float32)[None]


def root_matrix(noise, key, lowest, highest):
    key_diag, key_jitter, key_global = jax.random.split(key, 3)
    noise = noise * (0.5 / jnp.sqrt(jnp.float32(BS)))
    diag = jax.random.uniform(key_diag, (NBLK, BS), jnp.float32, 0.5, 1.5)
    position = jnp.arange(NBLK, dtype=jnp.float32) / NBLK
    ramp = 2.0 ** (position - 0.5)
    jitter = jax.random.uniform(key_jitter, (NBLK,), jnp.float32, 0.8, 1.25)
    overall = jnp.exp(jax.random.uniform(key_global, (), jnp.float32, jnp.log(lowest), jnp.log(highest)))
    scale = overall * ramp * jitter
    matrix = noise + diag[:, :, None] * jnp.eye(BS, dtype=jnp.float32)[None]
    return (matrix * scale[:, None, None]).astype(jnp.bfloat16)


def draw_left_stat(key, part):
    key = jax.random.fold_in(key, 21)
    key_off, key_diag = jax.random.split(key)
    noise = jax.random.normal(key_off, (NBLK, BS, BS), jnp.float32)
    return statistic(noise, key_diag)


def draw_right_stat(key, part):
    key = jax.random.fold_in(key, 31)
    key_off, key_diag = jax.random.split(key)
    noise = jax.random.normal(key_off, (NBLK, BS, BS), jnp.float32)
    return statistic(noise, key_diag)


def draw_left_root(key, part):
    key = jax.random.fold_in(key, 41)
    key_off, key_rest = jax.random.split(key)
    noise = jax.random.normal(key_off, (NBLK, BS, BS), jnp.float32)
    return root_matrix(noise, key_rest, 0.5, 1.0)


def draw_right_root(key, part):
    key = jax.random.fold_in(key, 51)
    key_off, key_rest = jax.random.split(key)
    noise = jax.random.normal(key_off, (NBLK, BS, BS), jnp.float32)
    return root_matrix(noise, key_rest, 0.5, 1.0)


def setup_inputs(seed: int = 0, part: int = 0) -> dict:
    keys = jax.random.split(jax.random.key(seed), 7)
    own_keys = jax.random.split(jax.random.fold_in(keys[6], part), 7)
    grad = draw_grad(jax.random.fold_in(jax.random.fold_in(keys[6], part), 71), part)
    left_stat = draw_left_stat(jax.random.fold_in(jax.random.fold_in(keys[6], part), 71), part)
    right_stat = draw_right_stat(jax.random.fold_in(jax.random.fold_in(keys[6], part), 71), part)
    left_root = draw_left_root(jax.random.fold_in(jax.random.fold_in(keys[6], part), 71), part)
    right_root = draw_right_root(jax.random.fold_in(jax.random.fold_in(keys[6], part), 71), part)
    table = jax.random.permutation(own_keys[5], NBLK).astype(jnp.int32)
    return dict(grad=grad, left_stat=left_stat, right_stat=right_stat, left_root=left_root, right_root=right_root, table=table)


stat_decay = 0.95
epsilon = 1e-06

def reference(grad, left_stat, right_stat, left_root, right_root, table):
    columns = D // BS
    blocks = grad.reshape(NBR, BS, columns, BS).transpose(0, 2, 1, 3).reshape(NBR * columns, BS, BS)
    chosen = jnp.take(blocks, table, axis=0)

    def per_slot(items):
        block, left, right, lroot, rroot = items
        gram_left = jnp.dot(block, block.T, preferred_element_type=jnp.float32)
        gram_right = jnp.dot(block.T, block, preferred_element_type=jnp.float32)
        left_out = stat_decay * left + (1.0 - stat_decay) / BS * gram_left
        right_out = stat_decay * right + (1.0 - stat_decay) / BS * gram_right
        half = jnp.dot(lroot, block, preferred_element_type=jnp.float32).astype(jnp.bfloat16)
        precond = jnp.dot(half, rroot, preferred_element_type=jnp.float32).astype(jnp.bfloat16)
        return (left_out, right_out, precond)
    left_new, right_new, precond = lax.map(per_slot, (chosen, left_stat, right_stat, left_root, right_root))
    pfloat = lax.optimization_barrier(precond).astype(jnp.float32)
    gfloat = grad.astype(jnp.float32)
    psum = jnp.sum(pfloat * pfloat)
    gsum = jnp.sum(gfloat * gfloat)
    ratio = jnp.sqrt(gsum / (psum + epsilon))
    scaled = (ratio * pfloat).astype(jnp.bfloat16)
    inverse = jnp.argsort(table).astype(jnp.int32)
    placed = jnp.take(scaled, inverse, axis=0)
    update = placed.reshape(NBR, columns, BS, BS).transpose(0, 2, 1, 3).reshape(NBR, BS, D)
    return (update, left_new, right_new)
```

```python
import jax
import jax.numpy as jnp
from jax import lax
from jax.experimental import pallas as pl
from jax.experimental.pallas import tpu as pltpu
from jax.sharding import PartitionSpec as P

stat_decay = 0.95
epsilon = 1e-06

DEVICES = 16
SLOTS = 2
ROWS = 32
BS = 512
COLUMNS = 16
LANES = 128
CHUNKS = BS // LANES
BODY = CHUNKS * SLOTS * ROWS
EXTRA = 16
VMEM_LIMIT = 48 * 1024 * 1024


def place(block):
    row = lax.div(block, COLUMNS)
    column = lax.rem(block, COLUMNS)
    return row, pl.ds(pl.multiple_of(column * BS, BS), BS)


def pack_kernel(table_ref, grad_ref, out_ref):
    for s in range(DEVICES * SLOTS):
        row, columns = place(table_ref[s])
        rows = slice(s % SLOTS * ROWS, (s % SLOTS + 1) * ROWS)
        out_ref[s // SLOTS, rows, :] = grad_ref[row, :, columns]


def pack(table, grad):
    return pl.pallas_call(
        pack_kernel,
        out_shape=jax.ShapeDtypeStruct((DEVICES, SLOTS * ROWS, BS), jnp.bfloat16),
        in_specs=[
            pl.BlockSpec(memory_space=pltpu.SMEM),
            pl.BlockSpec(memory_space=pltpu.VMEM),
        ],
        out_specs=pl.BlockSpec(memory_space=pltpu.VMEM),
        compiler_params=pltpu.CompilerParams(vmem_limit_bytes=VMEM_LIMIT),
        name="pack",
    )(table, grad)


def three_terms(value):
    value = 0.5 * value
    high = value.astype(jnp.bfloat16).astype(jnp.float32)
    rest = value - high
    middle = rest.astype(jnp.bfloat16).astype(jnp.float32)
    return high, middle, rest - middle


def precondition_kernel(owned_ref, lroot_ref, rroot_ref, out_ref):
    gpart = jnp.zeros((1, LANES), jnp.float32)
    ppart = jnp.zeros((1, LANES), jnp.float32)
    for t in range(SLOTS):
        rows = slice(t * ROWS, (t + 1) * ROWS)
        block = owned_ref[:, rows, :].reshape(BS, BS)
        half = jnp.dot(lroot_ref[t], block, preferred_element_type=jnp.float32)
        half = half.astype(jnp.bfloat16)
        precond = jnp.dot(half, rroot_ref[t], preferred_element_type=jnp.float32)
        precond = precond.astype(jnp.bfloat16)
        for q in range(CHUNKS):
            lanes = slice(q * LANES, (q + 1) * LANES)
            piece = precond[:, lanes]
            start = (q * SLOTS + t) * ROWS
            out_ref[:, start : start + ROWS, :] = piece.reshape(DEVICES, ROWS, LANES)
            pfloat = piece.astype(jnp.float32)
            ppart += jnp.sum(pfloat * pfloat, axis=0, keepdims=True)
            gfloat = block[:, lanes].astype(jnp.float32)
            gpart += jnp.sum(gfloat * gfloat, axis=0, keepdims=True)
    index = lax.broadcasted_iota(jnp.int32, (EXTRA, LANES), 0)
    tile = jnp.zeros((EXTRA, LANES), jnp.float32)
    for k, term in enumerate(three_terms(gpart) + three_terms(ppart)):
        tile = jnp.where(index == k, term, tile)
    tile = tile.astype(jnp.bfloat16)
    out_ref[:, BODY:, :] = jnp.broadcast_to(tile[None], (DEVICES, EXTRA, LANES))


def precondition(owned, left_root, right_root):
    return pl.pallas_call(
        precondition_kernel,
        out_shape=jax.ShapeDtypeStruct((DEVICES, BODY + EXTRA, LANES), jnp.bfloat16),
        in_specs=[pl.BlockSpec(memory_space=pltpu.VMEM)] * 3,
        out_specs=pl.BlockSpec(memory_space=pltpu.VMEM),
        compiler_params=pltpu.CompilerParams(vmem_limit_bytes=VMEM_LIMIT),
        cost_estimate=pl.CostEstimate(
            flops=4 * SLOTS * BS**3, bytes_accessed=8 * SLOTS * BS * BS, transcendentals=0
        ),
        name="precondition",
    )(owned, left_root, right_root)


PARTS = 2
PART = BS // PARTS


def statistics_kernel(owned_ref, left_ref, right_ref, left_out_ref, right_out_ref):
    rows = pl.ds(pl.multiple_of(pl.program_id(0) * ROWS, ROWS), ROWS)
    part = pl.program_id(1)
    share = DEVICES // PARTS
    block = owned_ref[:, rows, :].reshape(BS, BS)
    some_rows = owned_ref[pl.ds(part * share, share), rows, :].reshape(PART, BS)
    some_columns = owned_ref[:, rows, pl.ds(pl.multiple_of(part * PART, PART), PART)]
    some_columns = some_columns.reshape(BS, PART)
    weight = (1.0 - stat_decay) / BS
    gram = lax.dot_general(
        some_rows, block, (((1,), (1,)), ((), ())), preferred_element_type=jnp.float32
    )
    left_out_ref[0] = stat_decay * left_ref[0] + weight * gram
    gram = lax.dot_general(
        some_columns, block, (((0,), (0,)), ((), ())), preferred_element_type=jnp.float32
    )
    right_out_ref[0] = stat_decay * right_ref[0] + weight * gram


def statistics(owned, left_stat, right_stat):
    spec = pl.BlockSpec((1, PART, BS), lambda t, i: (t, i, 0))
    return pl.pallas_call(
        statistics_kernel,
        grid=(SLOTS, PARTS),
        out_shape=[jax.ShapeDtypeStruct((SLOTS, BS, BS), jnp.float32)] * 2,
        in_specs=[
            pl.BlockSpec((DEVICES, SLOTS * ROWS, BS), lambda t, i: (0, 0, 0)),
            spec,
            spec,
        ],
        out_specs=[spec, spec],
        compiler_params=pltpu.CompilerParams(vmem_limit_bytes=VMEM_LIMIT),
        cost_estimate=pl.CostEstimate(
            flops=4 * SLOTS * BS**3, bytes_accessed=18 * SLOTS * BS * BS, transcendentals=0
        ),
        name="statistics",
    )(owned, left_stat, right_stat)


def unpack_kernel(table_ref, back_ref, out_ref, scaled_ref, sem):
    extra = jnp.sum(back_ref[:, BODY:, :].astype(jnp.float32), axis=0)
    extra = 2.0 * jnp.sum(extra, axis=1, keepdims=True)
    gsum = extra[0:1] + extra[1:2] + extra[2:3]
    psum = extra[3:4] + extra[4:5] + extra[5:6]
    ratio = jnp.sqrt(gsum / (psum + epsilon))
    for s in range(DEVICES * SLOTS):
        for q in range(CHUNKS):
            start = (q * SLOTS + s % SLOTS) * ROWS
            pfloat = back_ref[s // SLOTS, start : start + ROWS, :].astype(jnp.float32)
            scaled_ref[s, :, q * LANES : (q + 1) * LANES] = (ratio * pfloat).astype(jnp.bfloat16)
        row, columns = place(table_ref[s])
        pltpu.make_async_copy(scaled_ref.at[s], out_ref.at[row, :, columns], sem).start()
    pltpu.make_async_copy(out_ref, out_ref, sem).wait()


def unpack(table, back):
    return pl.pallas_call(
        unpack_kernel,
        out_shape=jax.ShapeDtypeStruct((2, ROWS, COLUMNS * BS), jnp.bfloat16),
        in_specs=[
            pl.BlockSpec(memory_space=pltpu.SMEM),
            pl.BlockSpec(memory_space=pltpu.VMEM),
        ],
        out_specs=pl.BlockSpec(memory_space=pl.ANY),
        scratch_shapes=[
            pltpu.VMEM((DEVICES * SLOTS, ROWS, BS), jnp.bfloat16),
            pltpu.SemaphoreType.DMA,
        ],
        compiler_params=pltpu.CompilerParams(vmem_limit_bytes=VMEM_LIMIT),
        name="unpack",
    )(table, back)


def on_device(grad, left_stat, right_stat, left_root, right_root, table):
    outgoing = pack(table, grad)
    owned = lax.all_to_all(outgoing, "fsdp", split_axis=0, concat_axis=0, tiled=True)
    returning = precondition(owned, left_root, right_root)
    back = lax.all_to_all(returning, "fsdp", split_axis=0, concat_axis=0, tiled=True)
    left_new, right_new = statistics(owned, left_stat, right_stat)
    update = unpack(table, back)
    return (update, left_new, right_new)


def solution(mesh):
    return jax.shard_map(
        on_device,
        mesh=mesh,
        in_specs=(
            P("section", "fsdp", None),
            P(("section", "fsdp"), None, None),
            P(("section", "fsdp"), None, None),
            P(("section", "fsdp"), None, None),
            P(("section", "fsdp"), None, None),
            P("section"),
        ),
        out_specs=(
            P("section", "fsdp", None),
            P(("section", "fsdp"), None, None),
            P(("section", "fsdp"), None, None),
        ),
        check_vma=False,
    )
```

```python
import jax
import jax.numpy as jnp
from jax import lax
from jax.experimental import pallas as pl
from jax.experimental.pallas import tpu as pltpu
from jax.sharding import PartitionSpec as P

stat_decay = 0.95
epsilon = 1e-06

DEVICES = 16
SLOTS = 2
ROWS = 32
BS = 512
COLUMNS = 16
LANES = 128
CHUNKS = BS // LANES
BODY = CHUNKS * SLOTS * ROWS
EXTRA = 16
VMEM_LIMIT = 12 * 1024 * 1024
GRAD_PARTS = 4


def place(block):
    row = lax.div(block, COLUMNS)
    column = lax.rem(block, COLUMNS)
    return row, pl.ds(pl.multiple_of(column * BS, BS), BS)


def second_turn():
    return lax.rem(lax.axis_index("section"), 2) == 0


def pack_kernel(
    table_hbm, grad_hbm, right_hbm, out_ref, decayed_hbm,
    table_ref, slot_ref, grad_ref, stat_ref, table_sem, grad_sem, load_sem, store_sem,
):
    table_copy = pltpu.make_async_copy(table_hbm, table_ref, table_sem)
    table_copy.start()
    blocks = 2 * COLUMNS // GRAD_PARTS
    copies = []
    for part in range(GRAD_PARTS):
        row, column = divmod(part * blocks, COLUMNS)
        where = (row, slice(None), pl.ds(column * BS, blocks * BS))
        copies.append(
            pltpu.make_async_copy(grad_hbm.at[where], grad_ref.at[where], grad_sem.at[part])
        )
        copies[-1].start()
    table_copy.wait()
    for s in range(DEVICES * SLOTS):
        slot_ref[table_ref[s]] = s
    for block in range(2 * COLUMNS):
        if block % blocks == 0:
            copies[block // blocks].wait()
        row, column = divmod(block, COLUMNS)
        s = slot_ref[block]
        out_ref[lax.div(s, SLOTS), lax.rem(s, SLOTS)] = grad_ref[
            row, :, column * BS : (column + 1) * BS
        ]

    @pl.when(second_turn())
    def _():
        for t in range(SLOTS):
            load = pltpu.make_async_copy(right_hbm.at[t], stat_ref, load_sem)
            load.start()
            load.wait()
            stat_ref[...] = stat_decay * stat_ref[...]
            store = pltpu.make_async_copy(stat_ref, decayed_hbm.at[t], store_sem)
            store.start()
            store.wait()


def in_hbm(array):
    return pltpu.with_memory_space_constraint(array, pltpu.HBM)


def pack(table, grad, right_stat):
    return pl.pallas_call(
        pack_kernel,
        out_shape=[
            jax.ShapeDtypeStruct((DEVICES, SLOTS, ROWS, BS), jnp.bfloat16),
            pltpu.HBM((SLOTS, BS, BS), jnp.float32),
        ],
        in_specs=[pl.BlockSpec(memory_space=pl.ANY)] * 3,
        out_specs=[
            pl.BlockSpec(memory_space=pltpu.VMEM),
            pl.BlockSpec(memory_space=pl.ANY),
        ],
        scratch_shapes=[
            pltpu.SMEM((DEVICES * SLOTS,), jnp.int32),
            pltpu.SMEM((DEVICES * SLOTS,), jnp.int32),
            pltpu.VMEM((2, ROWS, COLUMNS * BS), jnp.bfloat16),
            pltpu.VMEM((BS, BS), jnp.float32),
            pltpu.SemaphoreType.DMA,
            pltpu.SemaphoreType.DMA((GRAD_PARTS,)),
            pltpu.SemaphoreType.DMA,
            pltpu.SemaphoreType.DMA,
        ],
        compiler_params=pltpu.CompilerParams(vmem_limit_bytes=VMEM_LIMIT),
        name="pack",
    )(*map(in_hbm, (table, grad, right_stat)))


def three_terms(value):
    value = 0.5 * value
    high = value.astype(jnp.bfloat16).astype(jnp.float32)
    rest = value - high
    middle = rest.astype(jnp.bfloat16).astype(jnp.float32)
    return high, middle, rest - middle


def precondition_kernel(owned_ref, lroot_ref, rroot_ref, out_hbm, out_ref, sem):
    gpart = jnp.zeros((1, LANES), jnp.float32)
    ppart = jnp.zeros((1, LANES), jnp.float32)
    copies = []
    for t in range(SLOTS):
        block = owned_ref[:, t].reshape(BS, BS)
        half = jnp.dot(lroot_ref[t], block, preferred_element_type=jnp.float32)
        half = half.astype(jnp.bfloat16)
        precond = jnp.dot(half, rroot_ref[t], preferred_element_type=jnp.float32)
        precond = precond.astype(jnp.bfloat16)
        for q in range(CHUNKS):
            lanes = slice(q * LANES, (q + 1) * LANES)
            piece = precond[:, lanes]
            start = (t * CHUNKS + q) * ROWS
            out_ref[:, start : start + ROWS, :] = piece.reshape(DEVICES, ROWS, LANES)
            pfloat = piece.astype(jnp.float32)
            ppart += jnp.sum(pfloat * pfloat, axis=0, keepdims=True)
            gfloat = block[:, lanes].astype(jnp.float32)
            gpart += jnp.sum(gfloat * gfloat, axis=0, keepdims=True)
        if t == SLOTS - 1:
            index = lax.broadcasted_iota(jnp.int32, (EXTRA, LANES), 0)
            tile = jnp.zeros((EXTRA, LANES), jnp.float32)
            for k, term in enumerate(three_terms(gpart) + three_terms(ppart)):
                tile = jnp.where(index == k, term, tile)
            tile = tile.astype(jnp.bfloat16)
            out_ref[:, BODY:, :] = jnp.broadcast_to(tile[None], (DEVICES, EXTRA, LANES))
        start = t * CHUNKS * ROWS
        rows = pl.ds(start, (CHUNKS * ROWS if t < SLOTS - 1 else BODY + EXTRA - start))
        copies.append(
            pltpu.make_async_copy(out_ref.at[:, rows], out_hbm.at[:, rows], sem.at[t])
        )
        copies[-1].start()
    for copy in copies:
        copy.wait()


def precondition(owned, left_root, right_root):
    shape = (DEVICES, BODY + EXTRA, LANES)
    return pl.pallas_call(
        precondition_kernel,
        out_shape=jax.ShapeDtypeStruct(shape, jnp.bfloat16),
        in_specs=[pl.BlockSpec(memory_space=pltpu.VMEM)] * 3,
        out_specs=pl.BlockSpec(memory_space=pl.ANY),
        scratch_shapes=[
            pltpu.VMEM(shape, jnp.bfloat16),
            pltpu.SemaphoreType.DMA((SLOTS,)),
        ],
        compiler_params=pltpu.CompilerParams(vmem_limit_bytes=VMEM_LIMIT),
        cost_estimate=pl.CostEstimate(
            flops=4 * SLOTS * BS**3, bytes_accessed=8 * SLOTS * BS * BS, transcendentals=0
        ),
        name="precondition",
    )(owned, left_root, right_root)


def statistics_kernel(
    owned_ref, left_hbm, right_hbm, decayed_hbm, left_out, right_out, stat_ref, load_sem, store_sem
):
    second = second_turn()
    loads = {}
    for t in range(SLOTS):
        for side, stat_hbm in enumerate((left_hbm, right_hbm)):
            where, sem = stat_ref.at[side, t], load_sem.at[side, t]
            loads[side, t] = pltpu.make_async_copy(stat_hbm.at[t], where, sem)
            if side == 0:
                loads[side, t].start()
            else:
                early = pltpu.make_async_copy(decayed_hbm.at[t], where, sem)
                pl.when(second)(early.start)
                pl.when(jnp.logical_not(second))(loads[side, t].start)
    decays = stat_decay, jnp.where(second, 1.0, stat_decay).astype(jnp.float32)
    weight = (1.0 - stat_decay) / BS
    stores = []
    for t in range(SLOTS):
        block = owned_ref[:, t].reshape(BS, BS)
        for side, out_hbm in enumerate((left_out, right_out)):
            dims = (((1 - side,), (1 - side,)), ((), ()))
            gram = lax.dot_general(block, block, dims, preferred_element_type=jnp.float32)
            loads[side, t].wait()
            stat_ref[side, t] = decays[side] * stat_ref[side, t] + weight * gram
            stores.append(
                pltpu.make_async_copy(stat_ref.at[side, t], out_hbm.at[t], store_sem.at[side, t])
            )
            stores[-1].start()
    for store in stores:
        store.wait()


def statistics(owned, left_stat, right_stat, decayed):
    return pl.pallas_call(
        statistics_kernel,
        out_shape=[jax.ShapeDtypeStruct((SLOTS, BS, BS), jnp.float32)] * 2,
        in_specs=[pl.BlockSpec(memory_space=pltpu.VMEM)] + [pl.BlockSpec(memory_space=pl.ANY)] * 3,
        out_specs=[pl.BlockSpec(memory_space=pltpu.HBM)] * 2,
        scratch_shapes=[
            pltpu.VMEM((2, SLOTS, BS, BS), jnp.float32),
            pltpu.SemaphoreType.DMA((2, SLOTS)),
            pltpu.SemaphoreType.DMA((2, SLOTS)),
        ],
        compiler_params=pltpu.CompilerParams(vmem_limit_bytes=VMEM_LIMIT),
        cost_estimate=pl.CostEstimate(
            flops=4 * SLOTS * BS**3, bytes_accessed=18 * SLOTS * BS * BS, transcendentals=0
        ),
        name="statistics",
    )(owned, *map(in_hbm, (left_stat, right_stat, decayed)))


def unpack_kernel(table_ref, back_ref, out_ref, scaled_ref, sem):
    extra = jnp.sum(back_ref[:, BODY:, :].astype(jnp.float32), axis=0)
    extra = 2.0 * jnp.sum(extra, axis=1, keepdims=True)
    gsum = extra[0:1] + extra[1:2] + extra[2:3]
    psum = extra[3:4] + extra[4:5] + extra[5:6]
    ratio = jnp.sqrt(gsum / (psum + epsilon))
    for s in range(DEVICES * SLOTS):
        for q in range(CHUNKS):
            start = (s % SLOTS * CHUNKS + q) * ROWS
            pfloat = back_ref[s // SLOTS, start : start + ROWS, :].astype(jnp.float32)
            scaled_ref[s, :, q * LANES : (q + 1) * LANES] = (ratio * pfloat).astype(jnp.bfloat16)
        row, columns = place(table_ref[s])
        pltpu.make_async_copy(scaled_ref.at[s], out_ref.at[row, :, columns], sem).start()
    pltpu.make_async_copy(out_ref, out_ref, sem).wait()


def unpack(table, back):
    return pl.pallas_call(
        unpack_kernel,
        out_shape=jax.ShapeDtypeStruct((2, ROWS, COLUMNS * BS), jnp.bfloat16),
        in_specs=[
            pl.BlockSpec(memory_space=pltpu.SMEM),
            pl.BlockSpec(memory_space=pltpu.VMEM),
        ],
        out_specs=pl.BlockSpec(memory_space=pl.ANY),
        scratch_shapes=[
            pltpu.VMEM((DEVICES * SLOTS, ROWS, BS), jnp.bfloat16),
            pltpu.SemaphoreType.DMA,
        ],
        compiler_params=pltpu.CompilerParams(vmem_limit_bytes=VMEM_LIMIT),
        name="unpack",
    )(table, back)


def on_device(grad, left_stat, right_stat, left_root, right_root, table):
    outgoing, decayed = pack(table, grad, right_stat)
    owned = lax.all_to_all(outgoing, "fsdp", split_axis=0, concat_axis=0, tiled=True)
    returning = precondition(owned, left_root, right_root)
    back = lax.all_to_all(returning, "fsdp", split_axis=0, concat_axis=0, tiled=True)
    left_new, right_new = statistics(owned, left_stat, right_stat, decayed)
    update = unpack(table, back)
    return (update, left_new, right_new)


def solution(mesh):
    return jax.shard_map(
        on_device,
        mesh=mesh,
        in_specs=(
            P("section", "fsdp", None),
            P(("section", "fsdp"), None, None),
            P(("section", "fsdp"), None, None),
            P(("section", "fsdp"), None, None),
            P(("section", "fsdp"), None, None),
            P("section"),
        ),
        out_specs=(
            P("section", "fsdp", None),
            P(("section", "fsdp"), None, None),
            P(("section", "fsdp"), None, None),
        ),
        check_vma=False,
    )
```

```python
import jax
import jax.numpy as jnp
from jax import lax
from jax.experimental import pallas as pl
from jax.experimental.pallas import tpu as pltpu
from jax.sharding import PartitionSpec as P

stat_decay = 0.95
epsilon = 1e-06

DEVICES = 16
SLOTS = 2
ROWS = 32
BS = 512
COLUMNS = 16
LANES = 128
CHUNKS = BS // LANES
BODY = CHUNKS * SLOTS * ROWS
EXTRA = 16
ORDER = [10, 11, 12, 13, 14, 15, 0, 1, 2, 3, 4, 5, 6, 7, 8, 9]
CHUNK = [ORDER.index(device) for device in range(DEVICES)]
VMEM_LIMIT = 12 * 1024 * 1024
GRAD_PARTS = 4


def place(block):
    row = lax.div(block, COLUMNS)
    column = lax.rem(block, COLUMNS)
    return row, pl.ds(pl.multiple_of(column * BS, BS), BS)


def second_turn():
    return lax.rem(lax.axis_index("section"), 2) == 0


def pack_kernel(
    table_hbm, grad_hbm, right_hbm, out_ref, decayed_hbm,
    table_ref, slot_ref, grad_ref, stat_ref, table_sem, grad_sem, load_sem, store_sem,
):
    table_copy = pltpu.make_async_copy(table_hbm, table_ref, table_sem)
    table_copy.start()
    blocks = 2 * COLUMNS // GRAD_PARTS
    copies = []
    for part in range(GRAD_PARTS):
        row, column = divmod(part * blocks, COLUMNS)
        where = (row, slice(None), pl.ds(column * BS, blocks * BS))
        copies.append(
            pltpu.make_async_copy(grad_hbm.at[where], grad_ref.at[where], grad_sem.at[part])
        )
        copies[-1].start()
    table_copy.wait()
    for s in range(DEVICES * SLOTS):
        slot_ref[table_ref[s]] = CHUNK[s // SLOTS] * SLOTS + s % SLOTS
    for block in range(2 * COLUMNS):
        if block % blocks == 0:
            copies[block // blocks].wait()
        row, column = divmod(block, COLUMNS)
        s = slot_ref[block]
        out_ref[lax.div(s, SLOTS), lax.rem(s, SLOTS)] = grad_ref[
            row, :, column * BS : (column + 1) * BS
        ]

    @pl.when(second_turn())
    def _():
        for t in range(SLOTS):
            load = pltpu.make_async_copy(right_hbm.at[t], stat_ref, load_sem)
            load.start()
            load.wait()
            stat_ref[...] = stat_decay * stat_ref[...]
            store = pltpu.make_async_copy(stat_ref, decayed_hbm.at[t], store_sem)
            store.start()
            store.wait()


def in_hbm(array):
    return pltpu.with_memory_space_constraint(array, pltpu.HBM)


def pack(table, grad, right_stat):
    return pl.pallas_call(
        pack_kernel,
        out_shape=[
            jax.ShapeDtypeStruct((DEVICES, SLOTS, ROWS, BS), jnp.bfloat16),
            pltpu.HBM((SLOTS, BS, BS), jnp.float32),
        ],
        in_specs=[pl.BlockSpec(memory_space=pl.ANY)] * 3,
        out_specs=[
            pl.BlockSpec(memory_space=pltpu.VMEM),
            pl.BlockSpec(memory_space=pl.ANY),
        ],
        scratch_shapes=[
            pltpu.SMEM((DEVICES * SLOTS,), jnp.int32),
            pltpu.SMEM((DEVICES * SLOTS,), jnp.int32),
            pltpu.VMEM((2, ROWS, COLUMNS * BS), jnp.bfloat16),
            pltpu.VMEM((BS, BS), jnp.float32),
            pltpu.SemaphoreType.DMA,
            pltpu.SemaphoreType.DMA((GRAD_PARTS,)),
            pltpu.SemaphoreType.DMA,
            pltpu.SemaphoreType.DMA,
        ],
        compiler_params=pltpu.CompilerParams(vmem_limit_bytes=VMEM_LIMIT),
        name="pack",
    )(*map(in_hbm, (table, grad, right_stat)))


def three_terms(value):
    value = 0.5 * value
    high = value.astype(jnp.bfloat16).astype(jnp.float32)
    rest = value - high
    middle = rest.astype(jnp.bfloat16).astype(jnp.float32)
    return high, middle, rest - middle


def whole_block(owned_ref, t):
    return jnp.concatenate([owned_ref[chunk, t] for chunk in CHUNK], axis=0)


def precondition_kernel(owned_ref, lroot_ref, rroot_ref, out_hbm, out_ref, sem):
    gpart = jnp.zeros((1, LANES), jnp.float32)
    ppart = jnp.zeros((1, LANES), jnp.float32)
    copies = []
    for t in range(SLOTS):
        block = whole_block(owned_ref, t)
        half = jnp.dot(lroot_ref[t], block, preferred_element_type=jnp.float32)
        half = half.astype(jnp.bfloat16)
        precond = jnp.dot(half, rroot_ref[t], preferred_element_type=jnp.float32)
        precond = precond.astype(jnp.bfloat16)
        for q in range(CHUNKS):
            lanes = slice(q * LANES, (q + 1) * LANES)
            piece = precond[:, lanes]
            start = (t * CHUNKS + q) * ROWS
            for device, chunk in enumerate(CHUNK):
                out_ref[chunk, start : start + ROWS, :] = piece[device * ROWS : (device + 1) * ROWS]
            pfloat = piece.astype(jnp.float32)
            ppart += jnp.sum(pfloat * pfloat, axis=0, keepdims=True)
            gfloat = block[:, lanes].astype(jnp.float32)
            gpart += jnp.sum(gfloat * gfloat, axis=0, keepdims=True)
        if t == SLOTS - 1:
            index = lax.broadcasted_iota(jnp.int32, (EXTRA, LANES), 0)
            tile = jnp.zeros((EXTRA, LANES), jnp.float32)
            for k, term in enumerate(three_terms(gpart) + three_terms(ppart)):
                tile = jnp.where(index == k, term, tile)
            tile = tile.astype(jnp.bfloat16)
            out_ref[:, BODY:, :] = jnp.broadcast_to(tile[None], (DEVICES, EXTRA, LANES))
        start = t * CHUNKS * ROWS
        rows = pl.ds(start, (CHUNKS * ROWS if t < SLOTS - 1 else BODY + EXTRA - start))
        copies.append(
            pltpu.make_async_copy(out_ref.at[:, rows], out_hbm.at[:, rows], sem.at[t])
        )
        copies[-1].start()
    for copy in copies:
        copy.wait()


def precondition(owned, left_root, right_root):
    shape = (DEVICES, BODY + EXTRA, LANES)
    return pl.pallas_call(
        precondition_kernel,
        out_shape=jax.ShapeDtypeStruct(shape, jnp.bfloat16),
        in_specs=[pl.BlockSpec(memory_space=pltpu.VMEM)] * 3,
        out_specs=pl.BlockSpec(memory_space=pl.ANY),
        scratch_shapes=[
            pltpu.VMEM(shape, jnp.bfloat16),
            pltpu.SemaphoreType.DMA((SLOTS,)),
        ],
        compiler_params=pltpu.CompilerParams(vmem_limit_bytes=VMEM_LIMIT),
        cost_estimate=pl.CostEstimate(
            flops=4 * SLOTS * BS**3, bytes_accessed=8 * SLOTS * BS * BS, transcendentals=0
        ),
        name="precondition",
    )(owned, left_root, right_root)


def statistics_kernel(
    owned_ref, left_hbm, right_hbm, decayed_hbm, left_out, right_out, stat_ref, load_sem, store_sem
):
    second = second_turn()
    loads = {}
    for t in range(SLOTS):
        for side, stat_hbm in enumerate((left_hbm, right_hbm)):
            where, sem = stat_ref.at[side, t], load_sem.at[side, t]
            loads[side, t] = pltpu.make_async_copy(stat_hbm.at[t], where, sem)
            if side == 0:
                loads[side, t].start()
            else:
                early = pltpu.make_async_copy(decayed_hbm.at[t], where, sem)
                pl.when(second)(early.start)
                pl.when(jnp.logical_not(second))(loads[side, t].start)
    decays = stat_decay, jnp.where(second, 1.0, stat_decay).astype(jnp.float32)
    weight = (1.0 - stat_decay) / BS
    stores = []
    for t in range(SLOTS):
        block = whole_block(owned_ref, t)
        for side, out_hbm in enumerate((left_out, right_out)):
            dims = (((1 - side,), (1 - side,)), ((), ()))
            gram = lax.dot_general(block, block, dims, preferred_element_type=jnp.float32)
            loads[side, t].wait()
            stat_ref[side, t] = decays[side] * stat_ref[side, t] + weight * gram
            stores.append(
                pltpu.make_async_copy(stat_ref.at[side, t], out_hbm.at[t], store_sem.at[side, t])
            )
            stores[-1].start()
    for store in stores:
        store.wait()


def statistics(owned, left_stat, right_stat, decayed):
    return pl.pallas_call(
        statistics_kernel,
        out_shape=[jax.ShapeDtypeStruct((SLOTS, BS, BS), jnp.float32)] * 2,
        in_specs=[pl.BlockSpec(memory_space=pltpu.VMEM)] + [pl.BlockSpec(memory_space=pl.ANY)] * 3,
        out_specs=[pl.BlockSpec(memory_space=pltpu.HBM)] * 2,
        scratch_shapes=[
            pltpu.VMEM((2, SLOTS, BS, BS), jnp.float32),
            pltpu.SemaphoreType.DMA((2, SLOTS)),
            pltpu.SemaphoreType.DMA((2, SLOTS)),
        ],
        compiler_params=pltpu.CompilerParams(vmem_limit_bytes=VMEM_LIMIT),
        cost_estimate=pl.CostEstimate(
            flops=4 * SLOTS * BS**3, bytes_accessed=18 * SLOTS * BS * BS, transcendentals=0
        ),
        name="statistics",
    )(owned, *map(in_hbm, (left_stat, right_stat, decayed)))


def unpack_kernel(table_ref, back_ref, out_ref, scaled_ref, sem):
    extra = jnp.sum(back_ref[:, BODY:, :].astype(jnp.float32), axis=0)
    extra = 2.0 * jnp.sum(extra, axis=1, keepdims=True)
    gsum = extra[0:1] + extra[1:2] + extra[2:3]
    psum = extra[3:4] + extra[4:5] + extra[5:6]
    ratio = jnp.sqrt(gsum / (psum + epsilon))
    for s in range(DEVICES * SLOTS):
        for q in range(CHUNKS):
            start = (s % SLOTS * CHUNKS + q) * ROWS
            pfloat = back_ref[CHUNK[s // SLOTS], start : start + ROWS, :].astype(jnp.float32)
            scaled_ref[s, :, q * LANES : (q + 1) * LANES] = (ratio * pfloat).astype(jnp.bfloat16)
        row, columns = place(table_ref[s])
        pltpu.make_async_copy(scaled_ref.at[s], out_ref.at[row, :, columns], sem).start()
    pltpu.make_async_copy(out_ref, out_ref, sem).wait()


def unpack(table, back):
    return pl.pallas_call(
        unpack_kernel,
        out_shape=jax.ShapeDtypeStruct((2, ROWS, COLUMNS * BS), jnp.bfloat16),
        in_specs=[
            pl.BlockSpec(memory_space=pltpu.SMEM),
            pl.BlockSpec(memory_space=pltpu.VMEM),
        ],
        out_specs=pl.BlockSpec(memory_space=pl.ANY),
        scratch_shapes=[
            pltpu.VMEM((DEVICES * SLOTS, ROWS, BS), jnp.bfloat16),
            pltpu.SemaphoreType.DMA,
        ],
        compiler_params=pltpu.CompilerParams(vmem_limit_bytes=VMEM_LIMIT),
        name="unpack",
    )(table, back)


def exchange(chunks):
    return lax.all_to_all(
        chunks, "fsdp", split_axis=0, concat_axis=0, axis_index_groups=[ORDER], tiled=True
    )


def on_device(grad, left_stat, right_stat, left_root, right_root, table):
    outgoing, decayed = pack(table, grad, right_stat)
    owned = exchange(outgoing)
    returning = precondition(owned, left_root, right_root)
    back = exchange(returning)
    left_new, right_new = statistics(owned, left_stat, right_stat, decayed)
    update = unpack(table, back)
    return (update, left_new, right_new)


def solution(mesh):
    return jax.shard_map(
        on_device,
        mesh=mesh,
        in_specs=(
            P("section", "fsdp", None),
            P(("section", "fsdp"), None, None),
            P(("section", "fsdp"), None, None),
            P(("section", "fsdp"), None, None),
            P(("section", "fsdp"), None, None),
            P("section"),
        ),
        out_specs=(
            P("section", "fsdp", None),
            P(("section", "fsdp"), None, None),
            P(("section", "fsdp"), None, None),
        ),
        check_vma=False,
    )
```

```python
import jax
import jax.numpy as jnp
from jax import lax
from jax.experimental import pallas as pl
from jax.experimental.pallas import tpu as pltpu
from jax.sharding import PartitionSpec as P

stat_decay = 0.95
epsilon = 1e-06

DEVICES = 16
SLOTS = 2
ROWS = 32
BS = 512
COLUMNS = 16
LANES = 128
CHUNKS = BS // LANES
BODY = CHUNKS * SLOTS * ROWS
EXTRA = 16
ORDER = [10, 11, 12, 13, 14, 15, 0, 1, 2, 3, 4, 5, 6, 7, 8, 9]
ORDER_BACK = [10, 11, 12, 13, 14, 15, 0, 1, 2, 3, 4, 5, 6, 7, 8, 9]
CHUNK = [ORDER.index(device) for device in range(DEVICES)]
CHUNK_BACK = [ORDER_BACK.index(device) for device in range(DEVICES)]
VMEM_LIMIT = 12 * 1024 * 1024
GRAD_PARTS = 4
EARLY = 384


def place(block):
    row = lax.div(block, COLUMNS)
    column = lax.rem(block, COLUMNS)
    return row, pl.ds(pl.multiple_of(column * BS, BS), BS)


def second_turn():
    return lax.rem(lax.axis_index("section"), 2) == 0


def pack_kernel(
    table_hbm, grad_hbm, right_hbm, out_ref, decayed_hbm,
    table_ref, slot_ref, grad_ref, stat_ref, table_sem, grad_sem, load_sem, store_sem,
):
    table_copy = pltpu.make_async_copy(table_hbm, table_ref, table_sem)
    table_copy.start()
    blocks = 2 * COLUMNS // GRAD_PARTS
    copies = []
    for part in range(GRAD_PARTS):
        row, column = divmod(part * blocks, COLUMNS)
        where = (row, slice(None), pl.ds(column * BS, blocks * BS))
        copies.append(
            pltpu.make_async_copy(grad_hbm.at[where], grad_ref.at[where], grad_sem.at[part])
        )
        copies[-1].start()
    table_copy.wait()
    for s in range(DEVICES * SLOTS):
        slot_ref[table_ref[s]] = CHUNK[s // SLOTS] * SLOTS + s % SLOTS
    for block in range(2 * COLUMNS):
        if block % blocks == 0:
            copies[block // blocks].wait()
        row, column = divmod(block, COLUMNS)
        s = slot_ref[block]
        out_ref[lax.div(s, SLOTS), lax.rem(s, SLOTS)] = grad_ref[
            row, :, column * BS : (column + 1) * BS
        ]

    @pl.when(second_turn())
    def _():
        for t in range(SLOTS):
            load = pltpu.make_async_copy(right_hbm.at[t, :EARLY], stat_ref, load_sem)
            load.start()
            load.wait()
            stat_ref[...] = stat_decay * stat_ref[...]
            store = pltpu.make_async_copy(stat_ref, decayed_hbm.at[t], store_sem)
            store.start()
            store.wait()


def in_hbm(array):
    return pltpu.with_memory_space_constraint(array, pltpu.HBM)


def pack(table, grad, right_stat):
    return pl.pallas_call(
        pack_kernel,
        out_shape=[
            jax.ShapeDtypeStruct((DEVICES, SLOTS, ROWS, BS), jnp.bfloat16),
            pltpu.HBM((SLOTS, EARLY, BS), jnp.float32),
        ],
        in_specs=[pl.BlockSpec(memory_space=pl.ANY)] * 3,
        out_specs=[
            pl.BlockSpec(memory_space=pltpu.VMEM),
            pl.BlockSpec(memory_space=pl.ANY),
        ],
        scratch_shapes=[
            pltpu.SMEM((DEVICES * SLOTS,), jnp.int32),
            pltpu.SMEM((DEVICES * SLOTS,), jnp.int32),
            pltpu.VMEM((2, ROWS, COLUMNS * BS), jnp.bfloat16),
            pltpu.VMEM((EARLY, BS), jnp.float32),
            pltpu.SemaphoreType.DMA,
            pltpu.SemaphoreType.DMA((GRAD_PARTS,)),
            pltpu.SemaphoreType.DMA,
            pltpu.SemaphoreType.DMA,
        ],
        compiler_params=pltpu.CompilerParams(vmem_limit_bytes=VMEM_LIMIT),
        name="pack",
    )(*map(in_hbm, (table, grad, right_stat)))


def three_terms(value):
    value = 0.5 * value
    high = value.astype(jnp.bfloat16).astype(jnp.float32)
    rest = value - high
    middle = rest.astype(jnp.bfloat16).astype(jnp.float32)
    return high, middle, rest - middle


def whole_block(owned_ref, t):
    return jnp.concatenate([owned_ref[chunk, t] for chunk in CHUNK], axis=0)


def precondition_kernel(owned_ref, lroot_ref, rroot_ref, out_hbm, out_ref, sem):
    gpart = jnp.zeros((1, LANES), jnp.float32)
    ppart = jnp.zeros((1, LANES), jnp.float32)
    copies = []
    for t in range(SLOTS):
        block = whole_block(owned_ref, t)
        half = jnp.dot(lroot_ref[t], block, preferred_element_type=jnp.float32)
        half = half.astype(jnp.bfloat16)
        precond = jnp.dot(half, rroot_ref[t], preferred_element_type=jnp.float32)
        precond = precond.astype(jnp.bfloat16)
        for q in range(CHUNKS):
            lanes = slice(q * LANES, (q + 1) * LANES)
            piece = precond[:, lanes]
            start = (t * CHUNKS + q) * ROWS
            for device, chunk in enumerate(CHUNK_BACK):
                out_ref[chunk, start : start + ROWS, :] = piece[device * ROWS : (device + 1) * ROWS]
            pfloat = piece.astype(jnp.float32)
            ppart += jnp.sum(pfloat * pfloat, axis=0, keepdims=True)
            gfloat = block[:, lanes].astype(jnp.float32)
            gpart += jnp.sum(gfloat * gfloat, axis=0, keepdims=True)
        if t == SLOTS - 1:
            index = lax.broadcasted_iota(jnp.int32, (EXTRA, LANES), 0)
            tile = jnp.zeros((EXTRA, LANES), jnp.float32)
            for k, term in enumerate(three_terms(gpart) + three_terms(ppart)):
                tile = jnp.where(index == k, term, tile)
            tile = tile.astype(jnp.bfloat16)
            out_ref[:, BODY:, :] = jnp.broadcast_to(tile[None], (DEVICES, EXTRA, LANES))
        start = t * CHUNKS * ROWS
        rows = pl.ds(start, (CHUNKS * ROWS if t < SLOTS - 1 else BODY + EXTRA - start))
        copies.append(
            pltpu.make_async_copy(out_ref.at[:, rows], out_hbm.at[:, rows], sem.at[t])
        )
        copies[-1].start()
    for copy in copies:
        copy.wait()


def precondition(owned, left_root, right_root):
    shape = (DEVICES, BODY + EXTRA, LANES)
    return pl.pallas_call(
        precondition_kernel,
        out_shape=jax.ShapeDtypeStruct(shape, jnp.bfloat16),
        in_specs=[pl.BlockSpec(memory_space=pltpu.VMEM)] * 3,
        out_specs=pl.BlockSpec(memory_space=pl.ANY),
        scratch_shapes=[
            pltpu.VMEM(shape, jnp.bfloat16),
            pltpu.SemaphoreType.DMA((SLOTS,)),
        ],
        compiler_params=pltpu.CompilerParams(vmem_limit_bytes=VMEM_LIMIT),
        cost_estimate=pl.CostEstimate(
            flops=4 * SLOTS * BS**3, bytes_accessed=8 * SLOTS * BS * BS, transcendentals=0
        ),
        name="precondition",
    )(owned, left_root, right_root)


def statistics_kernel(
    owned_ref, left_hbm, right_hbm, decayed_hbm, left_out, right_out, stat_ref, load_sem, store_sem
):
    second = second_turn()
    late = jnp.where(second, 1.0, stat_decay).astype(jnp.float32)
    weight = (1.0 - stat_decay) / BS
    top, bottom, whole = pl.ds(0, EARLY), pl.ds(EARLY, BS - EARLY), pl.ds(0, BS)
    pieces = ((left_hbm, whole, stat_decay),), ((right_hbm, top, late), (right_hbm, bottom, stat_decay))
    loads = {}
    for t in range(SLOTS):
        for side in range(2):
            for k, (stat_hbm, rows, _) in enumerate(pieces[side]):
                where, sem = stat_ref.at[side, t, rows], load_sem.at[side + k, t]
                load = pltpu.make_async_copy(stat_hbm.at[t, rows], where, sem)
                loads[side, t, k] = load
                if rows is top:
                    decayed = pltpu.make_async_copy(decayed_hbm.at[t], where, sem)
                    pl.when(second)(decayed.start)
                    pl.when(jnp.logical_not(second))(load.start)
                else:
                    load.start()
    stores = []
    for t in range(SLOTS):
        block = whole_block(owned_ref, t)
        for side, out_hbm in enumerate((left_out, right_out)):
            dims = (((1 - side,), (1 - side,)), ((), ()))
            gram = lax.dot_general(block, block, dims, preferred_element_type=jnp.float32)
            for k, (_, rows, decay) in enumerate(pieces[side]):
                loads[side, t, k].wait()
                new = gram[rows.start : rows.start + rows.size]
                stat_ref[side, t, rows] = decay * stat_ref[side, t, rows] + weight * new
            stores.append(
                pltpu.make_async_copy(stat_ref.at[side, t], out_hbm.at[t], store_sem.at[side, t])
            )
            stores[-1].start()
    for store in stores:
        store.wait()


def statistics(owned, left_stat, right_stat, decayed):
    return pl.pallas_call(
        statistics_kernel,
        out_shape=[jax.ShapeDtypeStruct((SLOTS, BS, BS), jnp.float32)] * 2,
        in_specs=[pl.BlockSpec(memory_space=pltpu.VMEM)] + [pl.BlockSpec(memory_space=pl.ANY)] * 3,
        out_specs=[pl.BlockSpec(memory_space=pltpu.HBM)] * 2,
        scratch_shapes=[
            pltpu.VMEM((2, SLOTS, BS, BS), jnp.float32),
            pltpu.SemaphoreType.DMA((3, SLOTS)),
            pltpu.SemaphoreType.DMA((2, SLOTS)),
        ],
        compiler_params=pltpu.CompilerParams(vmem_limit_bytes=VMEM_LIMIT),
        cost_estimate=pl.CostEstimate(
            flops=4 * SLOTS * BS**3, bytes_accessed=18 * SLOTS * BS * BS, transcendentals=0
        ),
        name="statistics",
    )(owned, *map(in_hbm, (left_stat, right_stat, decayed)))


def unpack_kernel(table_ref, back_ref, out_ref, scaled_ref, sem):
    extra = jnp.sum(back_ref[:, BODY:, :].astype(jnp.float32), axis=0)
    extra = 2.0 * jnp.sum(extra, axis=1, keepdims=True)
    gsum = extra[0:1] + extra[1:2] + extra[2:3]
    psum = extra[3:4] + extra[4:5] + extra[5:6]
    ratio = jnp.sqrt(gsum / (psum + epsilon))
    for s in range(DEVICES * SLOTS):
        for q in range(CHUNKS):
            start = (s % SLOTS * CHUNKS + q) * ROWS
            pfloat = back_ref[CHUNK_BACK[s // SLOTS], start : start + ROWS, :].astype(jnp.float32)
            scaled_ref[s, :, q * LANES : (q + 1) * LANES] = (ratio * pfloat).astype(jnp.bfloat16)
        row, columns = place(table_ref[s])
        pltpu.make_async_copy(scaled_ref.at[s], out_ref.at[row, :, columns], sem).start()
    pltpu.make_async_copy(out_ref, out_ref, sem).wait()


def unpack(table, back):
    return pl.pallas_call(
        unpack_kernel,
        out_shape=jax.ShapeDtypeStruct((2, ROWS, COLUMNS * BS), jnp.bfloat16),
        in_specs=[
            pl.BlockSpec(memory_space=pltpu.SMEM),
            pl.BlockSpec(memory_space=pltpu.VMEM),
        ],
        out_specs=pl.BlockSpec(memory_space=pl.ANY),
        scratch_shapes=[
            pltpu.VMEM((DEVICES * SLOTS, ROWS, BS), jnp.bfloat16),
            pltpu.SemaphoreType.DMA,
        ],
        compiler_params=pltpu.CompilerParams(vmem_limit_bytes=VMEM_LIMIT),
        name="unpack",
    )(table, back)


def exchange(chunks, order):
    return lax.all_to_all(
        chunks, "fsdp", split_axis=0, concat_axis=0, axis_index_groups=[order], tiled=True
    )


def on_device(grad, left_stat, right_stat, left_root, right_root, table):
    outgoing, decayed = pack(table, grad, right_stat)
    owned = exchange(outgoing, ORDER)
    returning = precondition(owned, left_root, right_root)
    back = exchange(returning, ORDER_BACK)
    left_new, right_new = statistics(owned, left_stat, right_stat, decayed)
    update = unpack(table, back)
    return (update, left_new, right_new)


def solution(mesh):
    return jax.shard_map(
        on_device,
        mesh=mesh,
        in_specs=(
            P("section", "fsdp", None),
            P(("section", "fsdp"), None, None),
            P(("section", "fsdp"), None, None),
            P(("section", "fsdp"), None, None),
            P(("section", "fsdp"), None, None),
            P("section"),
        ),
        out_specs=(
            P("section", "fsdp", None),
            P(("section", "fsdp"), None, None),
            P(("section", "fsdp"), None, None),
        ),
        check_vma=False,
    )
```

```python
import jax
import jax.numpy as jnp
from jax import lax
from jax.experimental import pallas as pl
from jax.experimental.pallas import tpu as pltpu
from jax.sharding import PartitionSpec as P

stat_decay = 0.95
epsilon = 1e-06

DEVICES = 16
SLOTS = 2
ROWS = 32
BS = 512
COLUMNS = 16
LANES = 128
CHUNKS = BS // LANES
BODY = CHUNKS * SLOTS * ROWS
EXTRA = 16
ORDER = [10, 11, 12, 13, 14, 15, 0, 1, 2, 3, 4, 5, 6, 7, 8, 9]
ORDER_BACK = [10, 11, 12, 13, 14, 15, 0, 1, 2, 3, 4, 5, 6, 7, 8, 9]
CHUNK = [ORDER.index(device) for device in range(DEVICES)]
CHUNK_BACK = [ORDER_BACK.index(device) for device in range(DEVICES)]
VMEM_LIMIT = 12 * 1024 * 1024
GRAD_PARTS = 4
EARLY = 384


def place(block):
    row = lax.div(block, COLUMNS)
    column = lax.rem(block, COLUMNS)
    return row, pl.ds(pl.multiple_of(column * BS, BS), BS)


def second_turn():
    return lax.rem(lax.axis_index("section"), 2) == 0


def pack_kernel(
    table_hbm, grad_hbm, right_hbm, out_ref, decayed_hbm,
    table_ref, slot_ref, grad_ref, stat_ref, table_sem, grad_sem, load_sem, store_sem,
):
    table_copy = pltpu.make_async_copy(table_hbm, table_ref, table_sem)
    table_copy.start()
    blocks = 2 * COLUMNS // GRAD_PARTS
    copies = []
    for part in range(GRAD_PARTS):
        row, column = divmod(part * blocks, COLUMNS)
        where = (row, slice(None), pl.ds(column * BS, blocks * BS))
        copies.append(
            pltpu.make_async_copy(grad_hbm.at[where], grad_ref.at[where], grad_sem.at[part])
        )
        copies[-1].start()
    table_copy.wait()
    for s in range(DEVICES * SLOTS):
        slot_ref[table_ref[s]] = CHUNK[s // SLOTS] * SLOTS + s % SLOTS
    for block in range(2 * COLUMNS):
        if block % blocks == 0:
            copies[block // blocks].wait()
        row, column = divmod(block, COLUMNS)
        s = slot_ref[block]
        out_ref[lax.div(s, SLOTS), lax.rem(s, SLOTS)] = grad_ref[
            row, :, column * BS : (column + 1) * BS
        ]

    @pl.when(second_turn())
    def _():
        for t in range(SLOTS):
            load = pltpu.make_async_copy(right_hbm.at[t, :EARLY], stat_ref, load_sem)
            load.start()
            load.wait()
            stat_ref[...] = stat_decay * stat_ref[...]
            store = pltpu.make_async_copy(stat_ref, decayed_hbm.at[t], store_sem)
            store.start()
            store.wait()


def in_hbm(array):
    return pltpu.with_memory_space_constraint(array, pltpu.HBM)


def pack(table, grad, right_stat):
    return pl.pallas_call(
        pack_kernel,
        out_shape=[
            jax.ShapeDtypeStruct((DEVICES, SLOTS, ROWS, BS), jnp.bfloat16),
            pltpu.HBM((SLOTS, EARLY, BS), jnp.float32),
        ],
        in_specs=[pl.BlockSpec(memory_space=pl.ANY)] * 3,
        out_specs=[
            pl.BlockSpec(memory_space=pltpu.VMEM),
            pl.BlockSpec(memory_space=pl.ANY),
        ],
        scratch_shapes=[
            pltpu.SMEM((DEVICES * SLOTS,), jnp.int32),
            pltpu.SMEM((DEVICES * SLOTS,), jnp.int32),
            pltpu.VMEM((2, ROWS, COLUMNS * BS), jnp.bfloat16),
            pltpu.VMEM((EARLY, BS), jnp.float32),
            pltpu.SemaphoreType.DMA,
            pltpu.SemaphoreType.DMA((GRAD_PARTS,)),
            pltpu.SemaphoreType.DMA,
            pltpu.SemaphoreType.DMA,
        ],
        compiler_params=pltpu.CompilerParams(vmem_limit_bytes=VMEM_LIMIT),
        cost_estimate=pl.CostEstimate(
            flops=SLOTS * EARLY * BS,
            bytes_accessed=4 * DEVICES * SLOTS * ROWS * BS + 8 * SLOTS * EARLY * BS,
            transcendentals=0,
        ),
        name="pack",
    )(*map(in_hbm, (table, grad, right_stat)))


def three_terms(value):
    value = 0.5 * value
    high = value.astype(jnp.bfloat16).astype(jnp.float32)
    rest = value - high
    middle = rest.astype(jnp.bfloat16).astype(jnp.float32)
    return high, middle, rest - middle


def whole_block(owned_ref, t):
    return jnp.concatenate([owned_ref[chunk, t] for chunk in CHUNK], axis=0)


def precondition_kernel(owned_ref, lroot_ref, rroot_ref, out_hbm, out_ref, sem):
    gpart = jnp.zeros((1, LANES), jnp.float32)
    ppart = jnp.zeros((1, LANES), jnp.float32)
    copies = []
    for t in range(SLOTS):
        block = whole_block(owned_ref, t)
        half = jnp.dot(lroot_ref[t], block, preferred_element_type=jnp.float32)
        half = half.astype(jnp.bfloat16)
        precond = jnp.dot(half, rroot_ref[t], preferred_element_type=jnp.float32)
        precond = precond.astype(jnp.bfloat16)
        for q in range(CHUNKS):
            lanes = slice(q * LANES, (q + 1) * LANES)
            piece = precond[:, lanes]
            start = (t * CHUNKS + q) * ROWS
            for device, chunk in enumerate(CHUNK_BACK):
                out_ref[chunk, start : start + ROWS, :] = piece[device * ROWS : (device + 1) * ROWS]
            pfloat = piece.astype(jnp.float32)
            ppart += jnp.sum(pfloat * pfloat, axis=0, keepdims=True)
            gfloat = block[:, lanes].astype(jnp.float32)
            gpart += jnp.sum(gfloat * gfloat, axis=0, keepdims=True)
        if t == SLOTS - 1:
            index = lax.broadcasted_iota(jnp.int32, (EXTRA, LANES), 0)
            tile = jnp.zeros((EXTRA, LANES), jnp.float32)
            for k, term in enumerate(three_terms(gpart) + three_terms(ppart)):
                tile = jnp.where(index == k, term, tile)
            tile = tile.astype(jnp.bfloat16)
            out_ref[:, BODY:, :] = jnp.broadcast_to(tile[None], (DEVICES, EXTRA, LANES))
        start = t * CHUNKS * ROWS
        rows = pl.ds(start, (CHUNKS * ROWS if t < SLOTS - 1 else BODY + EXTRA - start))
        copies.append(
            pltpu.make_async_copy(out_ref.at[:, rows], out_hbm.at[:, rows], sem.at[t])
        )
        copies[-1].start()
    for copy in copies:
        copy.wait()


def precondition(owned, left_root, right_root):
    shape = (DEVICES, BODY + EXTRA, LANES)
    return pl.pallas_call(
        precondition_kernel,
        out_shape=jax.ShapeDtypeStruct(shape, jnp.bfloat16),
        in_specs=[pl.BlockSpec(memory_space=pltpu.VMEM)] * 3,
        out_specs=pl.BlockSpec(memory_space=pl.ANY),
        scratch_shapes=[
            pltpu.VMEM(shape, jnp.bfloat16),
            pltpu.SemaphoreType.DMA((SLOTS,)),
        ],
        compiler_params=pltpu.CompilerParams(vmem_limit_bytes=VMEM_LIMIT),
        cost_estimate=pl.CostEstimate(
            flops=4 * SLOTS * BS**3, bytes_accessed=8 * SLOTS * BS * BS, transcendentals=0
        ),
        name="precondition",
    )(owned, left_root, right_root)


def statistics_kernel(
    owned_ref, left_hbm, right_hbm, decayed_hbm, left_out, right_out, stat_ref, load_sem, store_sem
):
    second = second_turn()
    late = jnp.where(second, 1.0, stat_decay).astype(jnp.float32)
    weight = (1.0 - stat_decay) / BS
    top, bottom, whole = pl.ds(0, EARLY), pl.ds(EARLY, BS - EARLY), pl.ds(0, BS)
    pieces = ((left_hbm, whole, stat_decay),), ((right_hbm, top, late), (right_hbm, bottom, stat_decay))
    loads = {}
    for t in range(SLOTS):
        for side in range(2):
            for k, (stat_hbm, rows, _) in enumerate(pieces[side]):
                where, sem = stat_ref.at[side, t, rows], load_sem.at[side + k, t]
                load = pltpu.make_async_copy(stat_hbm.at[t, rows], where, sem)
                loads[side, t, k] = load
                if rows is top:
                    decayed = pltpu.make_async_copy(decayed_hbm.at[t], where, sem)
                    pl.when(second)(decayed.start)
                    pl.when(jnp.logical_not(second))(load.start)
                else:
                    load.start()
    stores = []
    for t in range(SLOTS):
        block = whole_block(owned_ref, t)
        for side, out_hbm in enumerate((left_out, right_out)):
            dims = (((1 - side,), (1 - side,)), ((), ()))
            gram = lax.dot_general(block, block, dims, preferred_element_type=jnp.float32)
            for k, (_, rows, decay) in enumerate(pieces[side]):
                loads[side, t, k].wait()
                new = gram[rows.start : rows.start + rows.size]
                stat_ref[side, t, rows] = decay * stat_ref[side, t, rows] + weight * new
            stores.append(
                pltpu.make_async_copy(stat_ref.at[side, t], out_hbm.at[t], store_sem.at[side, t])
            )
            stores[-1].start()
    for store in stores:
        store.wait()


def statistics(owned, left_stat, right_stat, decayed):
    return pl.pallas_call(
        statistics_kernel,
        out_shape=[jax.ShapeDtypeStruct((SLOTS, BS, BS), jnp.float32)] * 2,
        in_specs=[pl.BlockSpec(memory_space=pltpu.VMEM)] + [pl.BlockSpec(memory_space=pl.ANY)] * 3,
        out_specs=[pl.BlockSpec(memory_space=pltpu.HBM)] * 2,
        scratch_shapes=[
            pltpu.VMEM((2, SLOTS, BS, BS), jnp.float32),
            pltpu.SemaphoreType.DMA((3, SLOTS)),
            pltpu.SemaphoreType.DMA((2, SLOTS)),
        ],
        compiler_params=pltpu.CompilerParams(vmem_limit_bytes=VMEM_LIMIT),
        cost_estimate=pl.CostEstimate(
            flops=4 * SLOTS * BS**3, bytes_accessed=18 * SLOTS * BS * BS, transcendentals=0
        ),
        name="statistics",
    )(owned, *map(in_hbm, (left_stat, right_stat, decayed)))


def unpack_kernel(table_ref, back_ref, out_ref, scaled_ref, sem):
    extra = jnp.sum(back_ref[:, BODY:, :].astype(jnp.float32), axis=0)
    extra = 2.0 * jnp.sum(extra, axis=1, keepdims=True)
    gsum = extra[0:1] + extra[1:2] + extra[2:3]
    psum = extra[3:4] + extra[4:5] + extra[5:6]
    ratio = jnp.sqrt(gsum / (psum + epsilon))
    for s in range(DEVICES * SLOTS):
        for q in range(CHUNKS):
            start = (s % SLOTS * CHUNKS + q) * ROWS
            pfloat = back_ref[CHUNK_BACK[s // SLOTS], start : start + ROWS, :].astype(jnp.float32)
            scaled_ref[s, :, q * LANES : (q + 1) * LANES] = (ratio * pfloat).astype(jnp.bfloat16)
        row, columns = place(table_ref[s])
        pltpu.make_async_copy(scaled_ref.at[s], out_ref.at[row, :, columns], sem).start()
    pltpu.make_async_copy(out_ref, out_ref, sem).wait()


def unpack(table, back):
    return pl.pallas_call(
        unpack_kernel,
        out_shape=jax.ShapeDtypeStruct((2, ROWS, COLUMNS * BS), jnp.bfloat16),
        in_specs=[
            pl.BlockSpec(memory_space=pltpu.SMEM),
            pl.BlockSpec(memory_space=pltpu.VMEM),
        ],
        out_specs=pl.BlockSpec(memory_space=pl.ANY),
        scratch_shapes=[
            pltpu.VMEM((DEVICES * SLOTS, ROWS, BS), jnp.bfloat16),
            pltpu.SemaphoreType.DMA,
        ],
        compiler_params=pltpu.CompilerParams(vmem_limit_bytes=VMEM_LIMIT),
        name="unpack",
    )(table, back)


def exchange(chunks, order):
    return lax.all_to_all(
        chunks, "fsdp", split_axis=0, concat_axis=0, axis_index_groups=[order], tiled=True
    )


def on_device(grad, left_stat, right_stat, left_root, right_root, table):
    outgoing, decayed = pack(table, grad, right_stat)
    owned = exchange(outgoing, ORDER)
    returning = precondition(owned, left_root, right_root)
    back = exchange(returning, ORDER_BACK)
    left_new, right_new = statistics(owned, left_stat, right_stat, decayed)
    update = unpack(table, back)
    return (update, left_new, right_new)


def solution(mesh):
    return jax.shard_map(
        on_device,
        mesh=mesh,
        in_specs=(
            P("section", "fsdp", None),
            P(("section", "fsdp"), None, None),
            P(("section", "fsdp"), None, None),
            P(("section", "fsdp"), None, None),
            P(("section", "fsdp"), None, None),
            P("section"),
        ),
        out_specs=(
            P("section", "fsdp", None),
            P(("section", "fsdp"), None, None),
            P(("section", "fsdp"), None, None),
        ),
        check_vma=False,
    )
```
